32 devices in a mesh: pts: 4 (over x, core), ctr: 8 (over z, y).
Axes of the slice: x: 2, y: 2, z: 4, core: 2. Of those that a mesh axis runs over, the one named last changes fastest.
Arguments:
- points: bfloat16 [32768, 128], P('pts'), may hold values from -16 to 16, as said below
- centers: bfloat16 [16384, 128], P('ctr'), may hold values from -16 to 16, as said below
- panel_inverse: bfloat16 [512, 512], P('pts'), as said below
- direction: float32 [32, 16384], P(None, 'ctr'), as said below
- residual: float32 [32, 16384], P(None, 'ctr'), as said below
Outputs:
- panel_rows: bfloat16 [16384, 512], P('ctr', 'pts')
- operator_image: float32 [32, 16384], P(None, 'ctr')
- new_residual: float32 [32, 16384], P(None, 'ctr')
The draws below stay inside these ranges and needn't reach their ends.
Inputs may be any that keep to these rules, and one draw needn't show every extreme that they name: `points`: rows of 128 real features. `centers`: rows of 128 real features. panel_inverse is lower triangular with a positive diagonal. `direction`: finite real values. `residual`: finite real values.
All inputs are finite; a program needn't handle non-finite values.
Results may differ from the reference program's by a relative error of at most 0.001.
The reference program's roundings to bfloat16 on the way count: a program that leaves them out, or rounds other values in their place, can miss the bound.
Values may be sent and summed in bfloat16 or wider, within the bound.
A program may use at most 128 MiB of HBM per device.

```python
import math
import jax
import jax.numpy as jnp
from jax import lax

D = 128
PANEL = 512
R = 32
M = 16384
NPOINTS = 32768


cluster_members = 64


def cluster_layout(key):
    group_count = M // cluster_members
    key_one, key_two = jax.random.split(jax.random.fold_in(key, 59))
    center_groups = (jax.random.permutation(key_one, M) // cluster_members).astype(jnp.int32)
    point_groups = jax.random.randint(key_two, (NPOINTS,), 0, group_count, dtype=jnp.int32)
    return (center_groups, point_groups)


def rising_values(key, salt_value, scale_value, coherent):
    key_one = jax.random.fold_in(jax.random.fold_in(key, salt_value), 0)
    key_two = jax.random.fold_in(jax.random.fold_in(key, salt_value), 1)
    key_four = jax.random.fold_in(jax.random.fold_in(key, salt_value), 3)
    position = jnp.arange(M, dtype=jnp.float32) / M
    rise_factor = jnp.exp(jnp.log(3.0) * position)[None, :]
    row_spread = jnp.exp(jax.random.uniform(key_four, (R, 1), jnp.float32) * jnp.log(10.0))
    base_draw = jnp.clip(jax.random.normal(key_one, (R, M), jnp.float32), -4.0, 4.0)
    spread = jnp.exp(jax.random.uniform(key_two, (1, M), jnp.float32) * jnp.log(10.0))
    values = base_draw * spread
    return scale_value * (values + coherent) * rise_factor * row_spread


def scattered_rows(key, salt_value, groups, row_count):
    group_count = M // cluster_members
    key_mean = jax.random.fold_in(key, 71)
    key_one = jax.random.fold_in(key, salt_value)
    means = 3.5 * jnp.clip(jax.random.normal(key_mean, (group_count, D), jnp.float32), -4.0, 4.0)
    jitter = 0.6 * jnp.clip(jax.random.normal(key_one, (row_count, D), jnp.float32), -4.0, 4.0)
    scattered = means[groups] + jitter
    return jnp.clip(scattered, -16.0, 16.0).astype(jnp.bfloat16)


def draw_points(key, part):
    center_groups, point_groups = cluster_layout(key)
    return scattered_rows(key, 83, point_groups, NPOINTS)


def draw_centers(key, part):
    center_groups, point_groups = cluster_layout(key)
    return scattered_rows(key, 97, center_groups, M)


def draw_direction(key, part):
    center_groups, point_groups = cluster_layout(key)
    group_count = M // cluster_members
    key_group = jax.random.fold_in(key, 13)
    group_part = 4.0 * jnp.clip(jax.random.normal(key_group, (R, group_count), jnp.float32), -3.0, 3.0)
    coherent = group_part[:, center_groups]
    return rising_values(key, 11, 2.0, coherent)


def draw_residual(key, part):
    return rising_values(key, 23, 0.1, jnp.zeros((R, M), jnp.float32))


def draw_panel_inverse(key, part):
    key_one, key_two = jax.random.split(jax.random.fold_in(key, 37))
    scale = 1.0 / (3.0 * jnp.sqrt(PANEL / 2.0))
    lower = jnp.clip(jax.random.normal(key_one, (PANEL, PANEL), jnp.float32), -4.0, 4.0)
    diagonal = jnp.exp(jax.random.uniform(key_two, (PANEL,), jnp.float32) * jnp.log(3.0))
    matrix = jnp.tril(lower, -1) + jnp.diag(diagonal)
    return (matrix * scale).astype(jnp.bfloat16)


def setup_inputs(seed: int = 0) -> dict:
    key_of = jax.random.split(jax.random.key(seed), 6)
    points = draw_points(jax.random.fold_in(key_of[5], 71), 0)
    centers = draw_centers(jax.random.fold_in(key_of[5], 71), 0)
    panel_inverse = draw_panel_inverse(jax.random.fold_in(key_of[5], 71), 0)
    direction = draw_direction(jax.random.fold_in(key_of[5], 71), 0)
    residual = draw_residual(jax.random.fold_in(key_of[5], 71), 0)
    return dict(points=points, centers=centers, panel_inverse=panel_inverse, direction=direction, residual=residual)


RIDGE_TERM = 0.002

def similarity(left, right):
    inner_terms = jnp.dot(left, right.T, preferred_element_type=jnp.float32)
    left_sq = lax.optimization_barrier(jnp.sum(jnp.square(left.astype(jnp.float32)), axis=1))
    right_sq = lax.optimization_barrier(jnp.sum(jnp.square(right.astype(jnp.float32)), axis=1))
    feature_count = left.shape[1]
    return jnp.exp(-(left_sq[:, None] + right_sq[None, :] - 2.0 * inner_terms) / (2.0 * feature_count))

def reference(points, centers, panel_inverse, direction, residual):
    head_rows = centers[:PANEL]
    head_vals = direction[:, :PANEL].astype(jnp.bfloat16)
    z1_full = jnp.dot(head_vals, panel_inverse.T, preferred_element_type=jnp.float32).astype(jnp.bfloat16)
    q_sum = jnp.dot(z1_full, panel_inverse, preferred_element_type=jnp.float32)
    q_bf16 = q_sum.astype(jnp.bfloat16)
    k_panel = similarity(centers, head_rows).astype(jnp.bfloat16)
    panel_rows = jnp.dot(k_panel, panel_inverse.T, preferred_element_type=jnp.float32).astype(jnp.bfloat16)
    correction = jnp.dot(q_bf16, k_panel.T, preferred_element_type=jnp.float32)
    columns = jnp.arange(M, dtype=jnp.int32)
    padded = jnp.concatenate([z1_full.astype(jnp.float32), jnp.zeros((R, M - PANEL), jnp.float32)], axis=1)
    z_vector = jnp.where(columns[None, :] < PANEL, padded, direction - correction)
    z_bf16 = z_vector.astype(jnp.bfloat16)
    block_rows = min(512, NPOINTS)
    w_scale = 1.0 / (2.0 * math.sqrt(M))
    image_scale = 1.0 / (2.0 * math.sqrt(NPOINTS))

    def accumulate(total, point_rows):
        kernel_rows = similarity(point_rows, centers).astype(jnp.bfloat16)
        w_full = jnp.dot(z_bf16, kernel_rows.T, preferred_element_type=jnp.float32) * w_scale
        w_bf16 = w_full.astype(jnp.bfloat16)
        return (total + jnp.dot(w_bf16, kernel_rows, preferred_element_type=jnp.float32), None)
    center_terms, unused = lax.scan(accumulate, jnp.zeros((R, M), jnp.float32), points.reshape(NPOINTS // block_rows, block_rows, D))
    operator_image = center_terms * image_scale + RIDGE_TERM * z_vector
    curvature = lax.optimization_barrier(jnp.sum(z_vector * operator_image, axis=1))
    r_squares = lax.optimization_barrier(jnp.sum(residual * residual, axis=1))
    new_residual = residual - (r_squares / curvature)[:, None] * operator_image
    return (panel_rows, operator_image, new_residual)
```

```python
import functools
import math

import jax
import jax.numpy as jnp
from jax import lax
from jax.experimental import pallas as pl
from jax.experimental.pallas import tpu as pltpu
from jax.sharding import PartitionSpec as P

RIDGE_TERM = 0.002
LINK = jnp.float32
NT = (((1,), (1,)), ((), ()))
F32 = jnp.float32
BF16 = jnp.bfloat16


def split_norms(rows):
    wide = rows.astype(F32)
    norms = jnp.sum(wide * wide, axis=1, keepdims=True)
    first = norms.astype(BF16).astype(F32)
    rest = norms - first
    second = rest.astype(BF16).astype(F32)
    return first, second, rest - second


def extended_left(rows):
    first, second, third = split_norms(rows)
    lane = lax.broadcasted_iota(jnp.int32, rows.shape, 1)
    ones = jnp.where(lane < 6, 1.0, 0.0)
    extra = jnp.where(
        lane == 0, first, jnp.where(lane == 1, second, jnp.where(lane == 2, third, ones))
    )
    return jnp.concatenate([rows, extra.astype(BF16)], axis=1)


def extended_right(rows):
    first, second, third = split_norms(rows)
    features = rows.shape[1]
    near, far = 1.0 / features, -0.5 / features
    lane = lax.broadcasted_iota(jnp.int32, rows.shape, 1)
    ones = jnp.where(lane < 3, far, 0.0)
    extra = jnp.where(
        lane == 3,
        first * far,
        jnp.where(lane == 4, second * far, jnp.where(lane == 5, third * far, ones)),
    )
    scaled = (rows.astype(F32) * near).astype(BF16)
    return jnp.concatenate([scaled, extra.astype(BF16)], axis=1)


def step(
    n_ctr, n_pts,
    points, centers, pinv, direction, residual,
    prow_out, image_out, resid_out,
    kmat, right_t, head_rows, head_vals, pfull, zvec, zlow,
    wsend, wrecv, wall, stat_send, stat_recv, img, irecv, oi, stat2_send, stat2_recv,
    head_sem, pin_send, pin_recv, w_send, w_recv, a_send, a_recv,
    s_send, s_recv, i_send, i_recv, o_send, o_recv, t_send, t_recv,
):
    ctr = lax.axis_index("ctr")
    pts = lax.axis_index("pts")
    m_dev, features = centers.shape
    npg = points.shape[0]
    share, panel = pinv.shape
    outputs = direction.shape[0]
    pieces = npg // n_ctr
    quarter = m_dev // n_pts
    w_scale = 1.0 / (2.0 * math.sqrt(m_dev * n_ctr))
    image_scale = 1.0 / (2.0 * math.sqrt(npg * n_pts))

    def ctr_peer(d):
        return lax.rem(ctr + d, n_ctr)

    def pts_peer(d):
        return lax.rem(pts + d, n_pts)

    def copy(src, dst, send_sem, recv_sem, axis, peer):
        return pltpu.make_async_remote_copy(
            src_ref=src, dst_ref=dst, send_sem=send_sem, recv_sem=recv_sem,
            device_id={axis: peer}, device_id_type=pl.DeviceIdType.MESH,
        )

    barrier = pltpu.get_barrier_semaphore()

    @pl.loop(1, n_ctr)
    def _(d):
        pl.semaphore_signal(
            barrier, inc=1, device_id={"ctr": ctr_peer(d)}, device_id_type=pl.DeviceIdType.MESH
        )

    @pl.loop(1, n_pts)
    def _(d):
        pl.semaphore_signal(
            barrier, inc=1, device_id={"pts": pts_peer(d)}, device_id_type=pl.DeviceIdType.MESH
        )

    pl.semaphore_wait(barrier, n_ctr + n_pts - 2)

    def vals_copy(peer):
        return copy(head_vals, head_vals, head_sem.at[0, peer], head_sem.at[2, 0], "ctr", peer)

    def rows_copy(peer):
        return copy(head_rows, head_rows, head_sem.at[1, peer], head_sem.at[3, 0], "ctr", peer)

    def pin_copy(slot, peer, recv_slot):
        return copy(pinv, pfull.at[slot], pin_send.at[peer], pin_recv.at[recv_slot], "pts", peer)

    @pl.when(ctr == 0)
    def _():
        head_vals[...] = direction[:, :panel].astype(BF16)
        head_rows[...] = centers[:panel, :]

        @pl.loop(1, n_ctr)
        def _(d):
            vals_copy(d).start()

        @pl.loop(1, n_ctr)
        def _(d):
            rows_copy(d).start()

    @pl.loop(1, n_pts)
    def _(d):
        pin_copy(pts, pts_peer(d), pts).start()

    pfull[pts] = pinv[...]

    tile_c = min(512, m_dev)
    for c in range(m_dev // tile_c):
        cols = slice(c * tile_c, (c + 1) * tile_c)
        right_t[:, cols] = extended_right(centers[cols, :]).astype(F32).T.astype(BF16)
    tile_p = min(256, npg)

    @pl.loop(0, npg // tile_p)
    def _(i):
        rows = pl.ds(pl.multiple_of(i * tile_p, tile_p), tile_p)
        left = extended_left(points[rows, :])
        for c in range(m_dev // tile_c):
            cols = slice(c * tile_c, (c + 1) * tile_c)
            kmat[rows, cols] = jnp.exp(
                jnp.dot(left, right_t[:, cols], preferred_element_type=F32)
            ).astype(BF16)

    @pl.when(ctr != 0)
    def _():
        vals_copy(0).wait_recv()
        rows_copy(0).wait_recv()

    @pl.loop(1, n_pts)
    def _(d):
        peer = pts_peer(d)
        pin_copy(peer, peer, peer).wait_recv()

    vals = head_vals[...]
    z1 = [
        lax.dot_general(vals, pfull[s], NT, preferred_element_type=F32).astype(BF16)
        for s in range(n_pts)
    ]
    q = sum(jnp.dot(z1[s], pfull[s], preferred_element_type=F32) for s in range(n_pts))
    q = q.astype(BF16)
    head_t = extended_right(head_rows[...]).astype(F32).T.astype(BF16)
    for c in range(m_dev // tile_c):
        cols = slice(c * tile_c, (c + 1) * tile_c)
        k_panel = jnp.exp(
            jnp.dot(extended_left(centers[cols, :]), head_t, preferred_element_type=F32)
        ).astype(BF16)
        prow_out[cols, :] = lax.dot_general(
            k_panel, pinv[...], NT, preferred_element_type=F32
        ).astype(BF16)
        zvec[:, cols] = direction[:, cols] - lax.dot_general(
            q, k_panel, NT, preferred_element_type=F32
        )

    @pl.when(ctr == 0)
    def _():
        for s in range(n_pts):
            zvec[:, s * share : (s + 1) * share] = z1[s].astype(F32)

    zlow[...] = zvec[...].astype(BF16)

    def piece_rows(j):
        return pl.ds(pl.multiple_of(j * pieces, pieces), pieces)

    def partial(j):
        return lax.dot_general(
            zlow[...], kmat[piece_rows(j), :], NT, preferred_element_type=F32
        )

    def w_copy(j, slot):
        return copy(wsend.at[j], wrecv.at[slot], w_send.at[j], w_recv.at[slot], "ctr", j)

    @pl.loop(1, n_ctr)
    def _(d):
        j = ctr_peer(d)
        wsend[j] = partial(j).astype(LINK)
        w_copy(j, ctr).start()

    wrecv[ctr] = partial(ctr).astype(LINK)

    z_squares = jnp.sum(zvec[...] * zvec[...], axis=1, keepdims=True)
    r_squares = jnp.sum(residual[...] * residual[...], axis=1, keepdims=True)

    @pl.loop(1, n_ctr)
    def _(d):
        j = ctr_peer(n_ctr - d)
        w_copy(j, j).wait_recv()

    owned = lax.fori_loop(
        1, n_ctr, lambda s, total: total + wrecv[s].astype(F32), wrecv[0].astype(F32)
    ) * w_scale
    owned_low = owned.astype(BF16)
    wall[ctr] = owned_low

    def a_copy(slot, peer):
        return copy(wall.at[slot], wall.at[slot], a_send.at[peer], a_recv.at[slot], "ctr", peer)

    @pl.loop(1, n_ctr)
    def _(d):
        a_copy(ctr, ctr_peer(d)).start()

    w_squares = jnp.sum(owned * owned_low.astype(F32), axis=1, keepdims=True)
    lane = lax.broadcasted_iota(jnp.int32, stat_send.shape, 1)
    stat_send[...] = jnp.where(
        lane == 0, w_squares, jnp.where(lane == 1, z_squares, jnp.where(lane == 2, r_squares, 0.0))
    )
    stat_recv[ctr] = stat_send[...]

    def s_copy(slot, peer):
        return copy(stat_send, stat_recv.at[slot], s_send.at[peer], s_recv.at[slot], "ctr", peer)

    @pl.loop(1, n_ctr)
    def _(d):
        s_copy(ctr, ctr_peer(d)).start()

    img[...] = jnp.dot(owned_low, kmat[piece_rows(ctr), :], preferred_element_type=F32)

    @pl.loop(1, n_ctr)
    def _(d):
        j = ctr_peer(n_ctr - d)
        a_copy(j, j).wait_recv()
        img[...] += jnp.dot(wall[j], kmat[piece_rows(j), :], preferred_element_type=F32)

    def quarter_cols(p):
        return pl.ds(pl.multiple_of(p * quarter, quarter), quarter)

    def i_copy(p, slot):
        return copy(
            img.at[:, quarter_cols(p)], irecv.at[slot], i_send.at[p], i_recv.at[slot], "pts", p
        )

    @pl.loop(1, n_pts)
    def _(d):
        i_copy(pts_peer(d), pts).start()

    @pl.loop(1, n_ctr)
    def _(d):
        j = ctr_peer(n_ctr - d)
        s_copy(j, j).wait_recv()

    stat_sum = lax.fori_loop(1, n_ctr, lambda s, total: total + stat_recv[s], stat_recv[0])
    stat2_send[...] = stat_sum
    stat2_recv[pts] = stat_sum

    def t_copy(slot, peer):
        return copy(stat2_send, stat2_recv.at[slot], t_send.at[peer], t_recv.at[slot], "pts", peer)

    @pl.loop(1, n_pts)
    def _(d):
        t_copy(pts, pts_peer(d)).start()

    irecv[pts] = img[:, quarter_cols(pts)]

    @pl.loop(1, n_pts)
    def _(d):
        j = pts_peer(d)
        i_copy(j, j).wait_recv()

    terms = irecv[0]
    for s in range(1, n_pts):
        terms = terms + irecv[s]
    oi[pts] = terms * image_scale + RIDGE_TERM * zvec[:, quarter_cols(pts)]

    def o_copy(slot, peer):
        return copy(oi.at[slot], oi.at[slot], o_send.at[peer], o_recv.at[slot], "pts", peer)

    @pl.loop(1, n_pts)
    def _(d):
        o_copy(pts, pts_peer(d)).start()

    @pl.loop(1, n_pts)
    def _(d):
        j = pts_peer(d)
        t_copy(j, j).wait_recv()

    w_total = stat2_recv[0][:, 0:1]
    for s in range(1, n_pts):
        w_total = w_total + stat2_recv[s][:, 0:1]
    curvature = image_scale / w_scale * w_total + RIDGE_TERM * stat_sum[:, 1:2]
    length = stat_sum[:, 2:3] / curvature

    @pl.loop(1, n_pts)
    def _(d):
        j = pts_peer(d)
        o_copy(j, j).wait_recv()

    for s in range(n_pts):
        cols = slice(s * quarter, (s + 1) * quarter)
        image_out[:, cols] = oi[s]
        resid_out[:, cols] = residual[:, cols] - length * oi[s]

    @pl.when(ctr == 0)
    def _():
        @pl.loop(1, n_ctr)
        def _(d):
            vals_copy(d).wait_send()
            rows_copy(d).wait_send()

    @pl.loop(1, n_ctr)
    def _(d):
        j = ctr_peer(d)
        w_copy(j, ctr).wait_send()
        a_copy(ctr, j).wait_send()
        s_copy(ctr, j).wait_send()

    @pl.loop(1, n_pts)
    def _(d):
        p = pts_peer(d)
        pin_copy(pts, p, pts).wait_send()
        i_copy(p, pts).wait_send()
        t_copy(pts, p).wait_send()
        o_copy(pts, p).wait_send()


def shards(n_ctr, n_pts, points, centers, panel_inverse, direction, residual):
    m_dev, features = centers.shape
    npg = points.shape[0]
    share, panel = panel_inverse.shape
    outputs = direction.shape[0]
    pieces = npg // n_ctr
    quarter = m_dev // n_pts
    vmem = pl.BlockSpec(memory_space=pltpu.VMEM)
    ctr_sem = pltpu.SemaphoreType.DMA((n_ctr,))
    pts_sem = pltpu.SemaphoreType.DMA((n_pts,))
    return pl.pallas_call(
        functools.partial(step, n_ctr, n_pts),
        out_shape=(
            jax.ShapeDtypeStruct((m_dev, share), BF16),
            jax.ShapeDtypeStruct((outputs, m_dev), F32),
            jax.ShapeDtypeStruct((outputs, m_dev), F32),
        ),
        in_specs=[vmem] * 5,
        out_specs=(vmem,) * 3,
        scratch_shapes=[
            pltpu.VMEM((npg, m_dev), BF16),
            pltpu.VMEM((2 * features, m_dev), BF16),
            pltpu.VMEM((panel, features), BF16),
            pltpu.VMEM((outputs, panel), BF16),
            pltpu.VMEM((n_pts, share, panel), BF16),
            pltpu.VMEM((outputs, m_dev), F32),
            pltpu.VMEM((outputs, m_dev), BF16),
            pltpu.VMEM((n_ctr, outputs, pieces), LINK),
            pltpu.VMEM((n_ctr, outputs, pieces), LINK),
            pltpu.VMEM((n_ctr, outputs, pieces), BF16),
            pltpu.VMEM((outputs, 128), F32),
            pltpu.VMEM((n_ctr, outputs, 128), F32),
            pltpu.VMEM((outputs, m_dev), F32),
            pltpu.VMEM((n_pts, outputs, quarter), F32),
            pltpu.VMEM((n_pts, outputs, quarter), F32),
            pltpu.VMEM((outputs, 128), F32),
            pltpu.VMEM((n_pts, outputs, 128), F32),
            pltpu.SemaphoreType.DMA((4, n_ctr)),
            pts_sem, pts_sem, ctr_sem, ctr_sem, ctr_sem, ctr_sem,
            ctr_sem, ctr_sem, pts_sem, pts_sem, pts_sem, pts_sem, pts_sem, pts_sem,
        ],
        compiler_params=pltpu.CompilerParams(
            collective_id=0, has_side_effects=True, vmem_limit_bytes=56 * 1024 * 1024
        ),
        cost_estimate=pl.CostEstimate(
            flops=2 * npg * m_dev * (2 * features + 2 * outputs),
            bytes_accessed=4 * npg * features,
            transcendentals=npg * m_dev,
        ),
    )(points, centers, panel_inverse, direction, residual)


def solution(mesh):
    n_ctr, n_pts = mesh.shape["ctr"], mesh.shape["pts"]
    in_specs = (P("pts", None), P("ctr", None), P("pts", None), P(None, "ctr"), P(None, "ctr"))
    out_specs = (P("ctr", "pts"), P(None, "ctr"), P(None, "ctr"))
    return jax.shard_map(
        functools.partial(shards, n_ctr, n_pts),
        mesh=mesh, in_specs=in_specs, out_specs=out_specs, check_vma=False,
    )
```

```python
import functools
import math

import jax
import jax.numpy as jnp
from jax import lax
from jax.experimental import pallas as pl
from jax.experimental.pallas import tpu as pltpu
from jax.sharding import PartitionSpec as P

RIDGE_TERM = 0.002
NT = (((1,), (1,)), ((), ()))
F32 = jnp.float32
BF16 = jnp.bfloat16


def split_norms(rows):
    wide = rows.astype(F32)
    norms = jnp.sum(wide * wide, axis=1, keepdims=True)
    first = norms.astype(BF16).astype(F32)
    rest = norms - first
    second = rest.astype(BF16).astype(F32)
    return first, second, rest - second


def extended_left(rows):
    first, second, third = split_norms(rows)
    lane = lax.broadcasted_iota(jnp.int32, rows.shape, 1)
    ones = jnp.where(lane < 6, 1.0, 0.0)
    extra = jnp.where(
        lane == 0, first, jnp.where(lane == 1, second, jnp.where(lane == 2, third, ones))
    )
    return jnp.concatenate([rows, extra.astype(BF16)], axis=1)


def extended_right(rows):
    first, second, third = split_norms(rows)
    features = rows.shape[1]
    near, far = 1.0 / features, -0.5 / features
    lane = lax.broadcasted_iota(jnp.int32, rows.shape, 1)
    ones = jnp.where(lane < 3, far, 0.0)
    extra = jnp.where(
        lane == 3,
        first * far,
        jnp.where(lane == 4, second * far, jnp.where(lane == 5, third * far, ones)),
    )
    scaled = (rows.astype(F32) * near).astype(BF16)
    return jnp.concatenate([scaled, extra.astype(BF16)], axis=1)


def step(
    n_ctr, n_pts,
    points, centers, pinv, direction, residual,
    prow_out, image_out, resid_out,
    kmat, right_t, head_rows, head_vals, pfull, k_panel, zvec, zlow,
    ysend, yrecv, own, zrecv, wall, stat_send, stat_recv, img, irecv, oi, stat2_send, stat2_recv,
    h_send, h_recv, g_send, g_recv, pin_send, pin_recv, y_send, y_recv, z_send, z_recv,
    m_send, az_send, af_send, a_recv,
    s_send, s_recv, i_send, i_recv, o_send, o_recv, t_send, t_recv,
):
    ctr = lax.axis_index("ctr")
    pts = lax.axis_index("pts")
    m_dev, features = centers.shape
    npg = points.shape[0]
    share, panel = pinv.shape
    outputs = direction.shape[0]
    pieces = npg // n_ctr
    quarter = m_dev // n_pts
    half = n_ctr // 2
    side = lax.rem(ctr, 2)
    group = lax.div(ctr, 2)
    mate = 2 * group + 1 - side
    w_scale = 1.0 / (2.0 * math.sqrt(m_dev * n_ctr))
    image_scale = 1.0 / (2.0 * math.sqrt(npg * n_pts))

    def ctr_peer(d):
        return lax.rem(ctr + d, n_ctr)

    def pts_peer(d):
        return lax.rem(pts + d, n_pts)

    def group_at(d):
        return lax.rem(group + d, half)

    def copy(src, dst, send_sem, recv_sem, axis, peer):
        return pltpu.make_async_remote_copy(
            src_ref=src, dst_ref=dst, send_sem=send_sem, recv_sem=recv_sem,
            device_id={axis: peer}, device_id_type=pl.DeviceIdType.MESH,
        )

    barrier = pltpu.get_barrier_semaphore()

    @pl.loop(1, n_ctr)
    def _(d):
        pl.semaphore_signal(
            barrier, inc=1, device_id={"ctr": ctr_peer(d)}, device_id_type=pl.DeviceIdType.MESH
        )

    @pl.loop(1, n_pts)
    def _(d):
        pl.semaphore_signal(
            barrier, inc=1, device_id={"pts": pts_peer(d)}, device_id_type=pl.DeviceIdType.MESH
        )

    pl.semaphore_wait(barrier, n_ctr + n_pts - 2)

    def vals_copy(peer):
        return copy(
            head_vals.at[pts], head_vals.at[pts], h_send.at[0, peer], h_recv.at[0], "ctr", peer
        )

    def rows_copy(peer):
        return copy(
            head_rows.at[pts], head_rows.at[pts], h_send.at[1, peer], h_recv.at[1], "ctr", peer
        )

    def vals_pass(slot, peer):
        return copy(
            head_vals.at[slot], head_vals.at[slot], g_send.at[0, peer], g_recv.at[0, slot],
            "pts", peer,
        )

    def rows_pass(slot, peer):
        return copy(
            head_rows.at[slot], head_rows.at[slot], g_send.at[1, peer], g_recv.at[1, slot],
            "pts", peer,
        )

    def pin_copy(slot, peer):
        return copy(pinv, pfull.at[slot], pin_send.at[peer], pin_recv.at[slot], "pts", peer)

    @pl.when(ctr == 0)
    def _():
        part = pl.ds(pl.multiple_of(pts * share, share), share)
        head_vals[pts] = direction[:, part].astype(BF16)
        head_rows[pts] = centers[part, :]

        @pl.loop(1, n_ctr)
        def _(d):
            vals_copy(d).start()
            rows_copy(d).start()

    @pl.loop(1, n_pts)
    def _(d):
        pin_copy(pts, pts_peer(d)).start()

    pfull[pts] = pinv[...]

    tile_r = min(512, m_dev)
    for c in range(m_dev // tile_r):
        cols = slice(c * tile_r, (c + 1) * tile_r)
        right_t[:, cols] = extended_right(centers[cols, :]).astype(F32).T.astype(BF16)
    tile_p, tile_c = min(512, 2 * pieces), min(256, m_dev)

    def build(t):
        @pl.loop(0, 2 * pieces // tile_p)
        def _(i):
            rows = pl.ds(pl.multiple_of(t * 2 * pieces + i * tile_p, tile_p), tile_p)
            left = extended_left(points[rows, :])
            for c in range(m_dev // tile_c):
                cols = slice(c * tile_c, (c + 1) * tile_c)
                kmat[rows, cols] = jnp.exp(
                    jnp.dot(left, right_t[:, cols], preferred_element_type=F32)
                ).astype(BF16)

    early = half // 2
    first = early // 2

    @pl.loop(0, first)
    def _(k):
        build(group_at(k + 1))

    @pl.when(ctr != 0)
    def _():
        vals_copy(0).wait_recv()
        rows_copy(0).wait_recv()

    @pl.loop(1, n_pts)
    def _(d):
        vals_pass(pts, pts_peer(d)).start()
        rows_pass(pts, pts_peer(d)).start()

    @pl.loop(first, early)
    def _(k):
        build(group_at(k + 1))

    @pl.loop(1, n_pts)
    def _(d):
        peer = pts_peer(d)
        pin_copy(peer, peer).wait_recv()
        vals_pass(peer, peer).wait_recv()
        rows_pass(peer, peer).wait_recv()

    vals = jnp.concatenate([head_vals[s] for s in range(n_pts)], axis=1)
    z1 = [
        lax.dot_general(vals, pfull[s], NT, preferred_element_type=F32).astype(BF16)
        for s in range(n_pts)
    ]
    q = sum(jnp.dot(z1[s], pfull[s], preferred_element_type=F32) for s in range(n_pts))
    q = q.astype(BF16)
    head_t = jnp.concatenate(
        [extended_right(head_rows[s]).astype(F32).T.astype(BF16) for s in range(n_pts)], axis=1
    )
    for c in range(m_dev // tile_r):
        cols = slice(c * tile_r, (c + 1) * tile_r)
        k_tile = jnp.exp(
            jnp.dot(extended_left(centers[cols, :]), head_t, preferred_element_type=F32)
        ).astype(BF16)
        k_panel[cols, :] = k_tile
        zvec[:, cols] = direction[:, cols] - lax.dot_general(
            q, k_tile, NT, preferred_element_type=F32
        )

    @pl.when(ctr == 0)
    def _():
        for s in range(n_pts):
            zvec[:, s * share : (s + 1) * share] = z1[s].astype(F32)

    zlow[...] = zvec[...].astype(BF16)

    def piece_rows(j):
        return pl.ds(pl.multiple_of(j * pieces, pieces), pieces)

    def partial(j):
        return lax.dot_general(
            zlow[...], kmat[piece_rows(j), :], NT, preferred_element_type=F32
        )

    def y_copy(t):
        return copy(ysend.at[t], yrecv.at[t], y_send.at[t], y_recv.at[t], "ctr", mate)

    def z_copy(t, slot):
        return copy(own.at[t], zrecv.at[slot], z_send.at[t], z_recv.at[slot], "ctr", 2 * t + side)

    def product(t):
        ysend[t] = partial(2 * t + 1 - side)
        y_copy(t).start()
        own[t] = partial(2 * t + side)

    def pass_on(t):
        y_copy(t).wait_recv()
        own[t] = own[t] + yrecv[t]
        z_copy(t, group).start()

    @pl.loop(0, early)
    def _(k):
        product(group_at(k + 1))

        @pl.when(k > 0)
        def _():
            pass_on(group_at(k))

    @pl.loop(early, half)
    def _(k):
        build(group_at(k + 1))
        product(group_at(k + 1))

        @pl.when(k > 0)
        def _():
            pass_on(group_at(k))

    z_squares = jnp.sum(zvec[...] * zvec[...], axis=1, keepdims=True)
    r_squares = jnp.sum(residual[...] * residual[...], axis=1, keepdims=True)
    y_copy(group).wait_recv()
    zrecv[group] = own[group] + yrecv[group]

    @pl.loop(1, half)
    def _(d):
        t = group_at(half - d)
        z_copy(t, t).wait_recv()

    owned = lax.fori_loop(1, half, lambda s, total: total + zrecv[s], zrecv[0]) * w_scale
    owned_low = owned.astype(BF16)
    wall[ctr] = owned_low

    def to_mate(j, sem):
        return copy(wall.at[j], wall.at[j], sem, a_recv.at[j], "ctr", mate)

    def to_group(j, t):
        return copy(wall.at[j], wall.at[j], az_send.at[t], a_recv.at[j], "ctr", 2 * t + side)

    @pl.loop(1, half)
    def _(d):
        to_group(ctr, group_at(d)).start()

    to_mate(ctr, m_send.at[0]).start()

    w_squares = jnp.sum(owned * owned_low.astype(F32), axis=1, keepdims=True)
    lane = lax.broadcasted_iota(jnp.int32, (outputs, 128), 1)
    stats = jnp.where(
        lane == 0, w_squares, jnp.where(lane == 1, z_squares, jnp.where(lane == 2, r_squares, 0.0))
    )
    stats = jnp.concatenate([stats, jnp.zeros((128 - outputs, 128), F32)], axis=0).T[:8, :]
    stat_send[...] = stats
    stat_recv[ctr] = stats

    def s_copy(slot, peer):
        return copy(stat_send, stat_recv.at[slot], s_send.at[peer], s_recv.at[slot], "ctr", peer)

    @pl.loop(1, n_ctr)
    def _(d):
        s_copy(ctr, ctr_peer(d)).start()

    img[...] = jnp.dot(owned_low, kmat[piece_rows(ctr), :], preferred_element_type=F32)

    @pl.loop(1, half)
    def _(d):
        t = group_at(half - d)
        j = 2 * t + side
        to_group(j, t).wait_recv()
        to_mate(j, af_send.at[t]).start()
        img[...] += jnp.dot(wall[j], kmat[piece_rows(j), :], preferred_element_type=F32)

    to_mate(mate, m_send.at[0]).wait_recv()
    img[...] += jnp.dot(wall[mate], kmat[piece_rows(mate), :], preferred_element_type=F32)

    @pl.loop(1, half)
    def _(d):
        t = group_at(half - d)
        to_mate(2 * t + 1 - side, af_send.at[t]).wait_recv()

    def quarter_cols(p):
        return pl.ds(pl.multiple_of(p * quarter, quarter), quarter)

    def i_copy(p, slot):
        return copy(
            img.at[:, quarter_cols(p)], irecv.at[slot], i_send.at[p], i_recv.at[slot], "pts", p
        )

    def rest(p):
        cols = quarter_cols(p)

        @pl.loop(1, half)
        def _(d):
            j = 2 * group_at(half - d) + 1 - side
            img[:, cols] += jnp.dot(wall[j], kmat[piece_rows(j), cols], preferred_element_type=F32)

    @pl.loop(1, n_pts)
    def _(d):
        p = pts_peer(d)
        rest(p)
        i_copy(p, pts).start()

    rest(pts)
    irecv[pts] = img[:, quarter_cols(pts)]

    @pl.loop(1, n_ctr)
    def _(d):
        j = ctr_peer(n_ctr - d)
        s_copy(j, j).wait_recv()

    stat_sum = lax.fori_loop(1, n_ctr, lambda s, total: total + stat_recv[s], stat_recv[0])
    stat2_send[...] = stat_sum
    stat2_recv[pts] = stat_sum

    def t_copy(slot, peer):
        return copy(stat2_send, stat2_recv.at[slot], t_send.at[peer], t_recv.at[slot], "pts", peer)

    @pl.loop(1, n_pts)
    def _(d):
        t_copy(pts, pts_peer(d)).start()

    @pl.loop(1, n_pts)
    def _(d):
        j = pts_peer(d)
        i_copy(j, j).wait_recv()

    terms = irecv[0]
    for s in range(1, n_pts):
        terms = terms + irecv[s]
    oi[pts] = terms * image_scale + RIDGE_TERM * zvec[:, quarter_cols(pts)]

    def o_copy(slot, peer):
        return copy(oi.at[slot], oi.at[slot], o_send.at[peer], o_recv.at[slot], "pts", peer)

    @pl.loop(1, n_pts)
    def _(d):
        o_copy(pts, pts_peer(d)).start()

    for c in range(m_dev // tile_r):
        cols = slice(c * tile_r, (c + 1) * tile_r)
        prow_out[cols, :] = lax.dot_general(
            k_panel[cols, :], pinv[...], NT, preferred_element_type=F32
        ).astype(BF16)

    @pl.loop(1, n_pts)
    def _(d):
        j = pts_peer(d)
        t_copy(j, j).wait_recv()

    w_total = stat2_recv[0][0:1, :]
    for s in range(1, n_pts):
        w_total = w_total + stat2_recv[s][0:1, :]
    curvature = image_scale / w_scale * w_total + RIDGE_TERM * stat_sum[1:2, :]
    length = stat_sum[2:3, :] / curvature
    length = jnp.broadcast_to(length, (128, 128)).T[:outputs, 0:1]

    @pl.loop(1, n_pts)
    def _(d):
        j = pts_peer(d)
        o_copy(j, j).wait_recv()

    for s in range(n_pts):
        cols = slice(s * quarter, (s + 1) * quarter)
        image_out[:, cols] = oi[s]
        resid_out[:, cols] = residual[:, cols] - length * oi[s]

    @pl.when(ctr == 0)
    def _():
        @pl.loop(1, n_ctr)
        def _(d):
            vals_copy(d).wait_send()
            rows_copy(d).wait_send()

    @pl.loop(1, half)
    def _(d):
        t = group_at(d)
        y_copy(t).wait_send()
        z_copy(t, group).wait_send()
        to_group(ctr, t).wait_send()
        to_mate(2 * t + side, af_send.at[t]).wait_send()

    y_copy(group).wait_send()
    to_mate(ctr, m_send.at[0]).wait_send()

    @pl.loop(1, n_ctr)
    def _(d):
        s_copy(ctr, ctr_peer(d)).wait_send()

    @pl.loop(1, n_pts)
    def _(d):
        p = pts_peer(d)
        vals_pass(pts, p).wait_send()
        rows_pass(pts, p).wait_send()
        pin_copy(pts, p).wait_send()
        i_copy(p, pts).wait_send()
        t_copy(pts, p).wait_send()
        o_copy(pts, p).wait_send()


def relay(*refs):
    count = len(refs) // 2
    for i in range(count):
        refs[count + i][...] = refs[i][...]


def shards(n_ctr, n_pts, points, centers, panel_inverse, direction, residual):
    m_dev, features = centers.shape
    npg = points.shape[0]
    share, panel = panel_inverse.shape
    outputs = direction.shape[0]
    pieces = npg // n_ctr
    quarter = m_dev // n_pts
    half = n_ctr // 2
    vmem = pl.BlockSpec(memory_space=pltpu.VMEM)
    dma = pltpu.SemaphoreType.DMA
    ctr_sem, pts_sem, half_sem = dma((n_ctr,)), dma((n_pts,)), dma((half,))
    piece_set = pltpu.VMEM((half, outputs, pieces), F32)
    out_shape = (
        jax.ShapeDtypeStruct((m_dev, share), BF16),
        jax.ShapeDtypeStruct((outputs, m_dev), F32),
        jax.ShapeDtypeStruct((outputs, m_dev), F32),
    )
    results = pl.pallas_call(
        functools.partial(step, n_ctr, n_pts),
        out_shape=out_shape,
        in_specs=[vmem] * 5,
        out_specs=(vmem,) * 3,
        scratch_shapes=[
            pltpu.VMEM((npg, m_dev), BF16),
            pltpu.VMEM((2 * features, m_dev), BF16),
            pltpu.VMEM((n_pts, share, features), BF16),
            pltpu.VMEM((n_pts, outputs, share), BF16),
            pltpu.VMEM((n_pts, share, panel), BF16),
            pltpu.VMEM((m_dev, panel), BF16),
            pltpu.VMEM((outputs, m_dev), F32),
            pltpu.VMEM((outputs, m_dev), BF16),
            piece_set, piece_set, piece_set, piece_set,
            pltpu.VMEM((n_ctr, outputs, pieces), BF16),
            pltpu.VMEM((8, 128), F32),
            pltpu.VMEM((n_ctr, 8, 128), F32),
            pltpu.VMEM((outputs, m_dev), F32),
            pltpu.VMEM((n_pts, outputs, quarter), F32),
            pltpu.VMEM((n_pts, outputs, quarter), F32),
            pltpu.VMEM((8, 128), F32),
            pltpu.VMEM((n_pts, 8, 128), F32),
            dma((2, n_ctr)), dma((2,)), dma((2, n_pts)), dma((2, n_pts)), pts_sem, pts_sem,
            half_sem, half_sem, half_sem, half_sem, dma((1,)), half_sem, half_sem, ctr_sem,
            ctr_sem, ctr_sem, pts_sem, pts_sem, pts_sem, pts_sem, pts_sem, pts_sem,
        ],
        compiler_params=pltpu.CompilerParams(
            collective_id=0, has_side_effects=True, vmem_limit_bytes=56 * 1024 * 1024
        ),
        cost_estimate=pl.CostEstimate(
            flops=2 * npg * m_dev * (2 * features + 2 * outputs),
            bytes_accessed=4 * npg * features,
            transcendentals=npg * m_dev,
        ),
    )(points, centers, panel_inverse, direction, residual)
    return pl.pallas_call(
        relay,
        out_shape=out_shape,
        in_specs=[vmem] * 3,
        out_specs=(vmem,) * 3,
    )(*results)


def solution(mesh):
    n_ctr, n_pts = mesh.shape["ctr"], mesh.shape["pts"]
    in_specs = (P("pts", None), P("ctr", None), P("pts", None), P(None, "ctr"), P(None, "ctr"))
    out_specs = (P("ctr", "pts"), P(None, "ctr"), P(None, "ctr"))
    return jax.shard_map(
        functools.partial(shards, n_ctr, n_pts),
        mesh=mesh, in_specs=in_specs, out_specs=out_specs, check_vma=False,
    )
```

```python
import functools
import math

import jax
import jax.numpy as jnp
from jax import lax
from jax.experimental import pallas as pl
from jax.experimental.pallas import tpu as pltpu
from jax.sharding import PartitionSpec as P

RIDGE_TERM = 0.002
NT = (((1,), (1,)), ((), ()))
F32 = jnp.float32
BF16 = jnp.bfloat16


def split_norms(rows):
    wide = rows.astype(F32)
    norms = jnp.sum(wide * wide, axis=1, keepdims=True)
    first = norms.astype(BF16).astype(F32)
    rest = norms - first
    second = rest.astype(BF16).astype(F32)
    return first, second, rest - second


def extended_left(rows):
    first, second, third = split_norms(rows)
    lane = lax.broadcasted_iota(jnp.int32, rows.shape, 1)
    ones = jnp.where(lane < 6, 1.0, 0.0)
    extra = jnp.where(
        lane == 0, first, jnp.where(lane == 1, second, jnp.where(lane == 2, third, ones))
    )
    return jnp.concatenate([rows, extra.astype(BF16)], axis=1)


def extended_right(rows):
    first, second, third = split_norms(rows)
    features = rows.shape[1]
    near, far = 1.0 / features, -0.5 / features
    lane = lax.broadcasted_iota(jnp.int32, rows.shape, 1)
    ones = jnp.where(lane < 3, far, 0.0)
    extra = jnp.where(
        lane == 3,
        first * far,
        jnp.where(lane == 4, second * far, jnp.where(lane == 5, third * far, ones)),
    )
    scaled = (rows.astype(F32) * near).astype(BF16)
    return jnp.concatenate([scaled, extra.astype(BF16)], axis=1)


def step(
    n_ctr, n_pts,
    points, centers, pinv, direction, residual,
    prow_out, image_out, resid_out,
    kmat, right_t, head_rows, head_vals, pfull, k_panel, zvec, zlow,
    ysend, yrecv, own, zsend, zrecv, wall, stat_send, stat_recv, img, irecv, oi, stat2_send, stat2_recv,
    h_send, h_recv, g_send, g_recv, pin_send, pin_recv, y_send, y_recv, z_send, z_recv,
    m_send, az_send, af_send, a_recv,
    s_send, s_recv, i_send, i_recv, o_send, o_recv, t_send, t_recv,
):
    ctr = lax.axis_index("ctr")
    pts = lax.axis_index("pts")
    m_dev, features = centers.shape
    npg = points.shape[0]
    share, panel = pinv.shape
    outputs = direction.shape[0]
    pieces = npg // n_ctr
    quarter = m_dev // n_pts
    half = n_ctr // 2
    side = lax.rem(ctr, 2)
    group = lax.div(ctr, 2)
    mate = 2 * group + 1 - side
    w_scale = 1.0 / (2.0 * math.sqrt(m_dev * n_ctr))
    image_scale = 1.0 / (2.0 * math.sqrt(npg * n_pts))

    def ctr_peer(d):
        return lax.rem(ctr + d, n_ctr)

    def pts_peer(d):
        return lax.rem(pts + d, n_pts)

    def group_at(d):
        return lax.rem(group + d, half)

    def copy(src, dst, send_sem, recv_sem, axis, peer):
        return pltpu.make_async_remote_copy(
            src_ref=src, dst_ref=dst, send_sem=send_sem, recv_sem=recv_sem,
            device_id={axis: peer}, device_id_type=pl.DeviceIdType.MESH,
        )

    barrier = pltpu.get_barrier_semaphore()

    @pl.loop(1, n_ctr)
    def _(d):
        pl.semaphore_signal(
            barrier, inc=1, device_id={"ctr": ctr_peer(d)}, device_id_type=pl.DeviceIdType.MESH
        )

    @pl.loop(1, n_pts)
    def _(d):
        pl.semaphore_signal(
            barrier, inc=1, device_id={"pts": pts_peer(d)}, device_id_type=pl.DeviceIdType.MESH
        )

    pl.semaphore_wait(barrier, n_ctr + n_pts - 2)

    def vals_copy(peer):
        return copy(
            head_vals.at[pts], head_vals.at[pts], h_send.at[0, peer], h_recv.at[0], "ctr", peer
        )

    def rows_copy(peer):
        return copy(
            head_rows.at[pts], head_rows.at[pts], h_send.at[1, peer], h_recv.at[1], "ctr", peer
        )

    def vals_pass(slot, peer):
        return copy(
            head_vals.at[slot], head_vals.at[slot], g_send.at[0, peer], g_recv.at[0, slot],
            "pts", peer,
        )

    def rows_pass(slot, peer):
        return copy(
            head_rows.at[slot], head_rows.at[slot], g_send.at[1, peer], g_recv.at[1, slot],
            "pts", peer,
        )

    def pin_copy(slot, peer):
        return copy(pinv, pfull.at[slot], pin_send.at[peer], pin_recv.at[slot], "pts", peer)

    @pl.when(ctr == 0)
    def _():
        part = pl.ds(pl.multiple_of(pts * share, share), share)
        head_vals[pts] = direction[:, part].astype(BF16)
        head_rows[pts] = centers[part, :]

        @pl.loop(1, n_ctr)
        def _(d):
            vals_copy(d).start()
            rows_copy(d).start()

    @pl.loop(1, n_pts)
    def _(d):
        pin_copy(pts, pts_peer(d)).start()

    pfull[pts] = pinv[...]

    tile_r = min(512, m_dev)
    for c in range(m_dev // tile_r):
        cols = slice(c * tile_r, (c + 1) * tile_r)
        right_t[:, cols] = extended_right(centers[cols, :]).astype(F32).T.astype(BF16)
    tile_p, tile_c = min(512, 2 * pieces), min(256, m_dev)

    def build(t):
        @pl.loop(0, 2 * pieces // tile_p)
        def _(i):
            rows = pl.ds(pl.multiple_of(t * 2 * pieces + i * tile_p, tile_p), tile_p)
            left = extended_left(points[rows, :])
            for c in range(m_dev // tile_c):
                cols = slice(c * tile_c, (c + 1) * tile_c)
                kmat[rows, cols] = jnp.exp(
                    jnp.dot(left, right_t[:, cols], preferred_element_type=F32)
                ).astype(BF16)

    early = max(half - half // 4, 1)
    first = (early + 1) // 2

    @pl.loop(0, first)
    def _(k):
        build(group_at(k + 1))

    @pl.when(ctr != 0)
    def _():
        vals_copy(0).wait_recv()
        rows_copy(0).wait_recv()

    @pl.loop(1, n_pts)
    def _(d):
        vals_pass(pts, pts_peer(d)).start()
        rows_pass(pts, pts_peer(d)).start()

    @pl.loop(first, early)
    def _(k):
        build(group_at(k + 1))

    @pl.loop(1, n_pts)
    def _(d):
        peer = pts_peer(d)
        pin_copy(peer, peer).wait_recv()
        vals_pass(peer, peer).wait_recv()
        rows_pass(peer, peer).wait_recv()

    vals = jnp.concatenate([head_vals[s] for s in range(n_pts)], axis=1)
    z1 = [
        lax.dot_general(vals, pfull[s], NT, preferred_element_type=F32).astype(BF16)
        for s in range(n_pts)
    ]
    q = sum(jnp.dot(z1[s], pfull[s], preferred_element_type=F32) for s in range(n_pts))
    q = q.astype(BF16)
    head_t = jnp.concatenate(
        [extended_right(head_rows[s]).astype(F32).T.astype(BF16) for s in range(n_pts)], axis=1
    )
    for c in range(m_dev // tile_r):
        cols = slice(c * tile_r, (c + 1) * tile_r)
        k_tile = jnp.exp(
            jnp.dot(extended_left(centers[cols, :]), head_t, preferred_element_type=F32)
        ).astype(BF16)
        k_panel[cols, :] = k_tile
        zvec[:, cols] = direction[:, cols] - lax.dot_general(
            q, k_tile, NT, preferred_element_type=F32
        )

    @pl.when(ctr == 0)
    def _():
        for s in range(n_pts):
            zvec[:, s * share : (s + 1) * share] = z1[s].astype(F32)

    zlow[...] = zvec[...].astype(BF16)

    def piece_rows(j):
        return pl.ds(pl.multiple_of(j * pieces, pieces), pieces)

    def partial(j):
        return lax.dot_general(
            zlow[...], kmat[piece_rows(j), :], NT, preferred_element_type=F32
        )

    def y_copy(t):
        return copy(ysend.at[t], yrecv.at[t], y_send.at[t], y_recv.at[t], "ctr", mate)

    def z_copy(t, slot):
        return copy(zsend.at[t], zrecv.at[slot], z_send.at[t], z_recv.at[slot], "ctr", 2 * t + side)

    def product(t):
        ysend[t] = partial(2 * t + 1 - side).astype(BF16)
        y_copy(t).start()
        own[t] = partial(2 * t + side)

    def pass_on(t):
        y_copy(t).wait_recv()
        zsend[t] = (own[t] + yrecv[t].astype(F32)).astype(BF16)
        z_copy(t, group).start()

    @pl.loop(0, early)
    def _(k):
        product(group_at(k + 1))

        @pl.when(k > 0)
        def _():
            pass_on(group_at(k))

    @pl.loop(early, half)
    def _(k):
        build(group_at(k + 1))
        product(group_at(k + 1))

        @pl.when(k > 0)
        def _():
            pass_on(group_at(k))

    z_squares = jnp.sum(zvec[...] * zvec[...], axis=1, keepdims=True)
    r_squares = jnp.sum(residual[...] * residual[...], axis=1, keepdims=True)
    y_copy(group).wait_recv()

    @pl.loop(1, half)
    def _(d):
        t = group_at(half - d)
        z_copy(t, t).wait_recv()

    owned = lax.fori_loop(
        1,
        half,
        lambda d, total: total + zrecv[group_at(d)].astype(F32),
        own[group] + yrecv[group].astype(F32),
    ) * w_scale
    owned_low = owned.astype(BF16)
    wall[ctr] = owned_low

    def to_mate(j, sem):
        return copy(wall.at[j], wall.at[j], sem, a_recv.at[j], "ctr", mate)

    def to_group(j, t):
        return copy(wall.at[j], wall.at[j], az_send.at[t], a_recv.at[j], "ctr", 2 * t + side)

    @pl.loop(1, half)
    def _(d):
        to_group(ctr, group_at(d)).start()

    to_mate(ctr, m_send.at[0]).start()

    w_squares = jnp.sum(owned * owned_low.astype(F32), axis=1, keepdims=True)
    lane = lax.broadcasted_iota(jnp.int32, (outputs, 128), 1)
    stats = jnp.where(
        lane == 0, w_squares, jnp.where(lane == 1, z_squares, jnp.where(lane == 2, r_squares, 0.0))
    )
    stats = jnp.concatenate([stats, jnp.zeros((128 - outputs, 128), F32)], axis=0).T[:8, :]
    stat_send[...] = stats
    stat_recv[ctr] = stats

    def s_copy(slot, peer):
        return copy(stat_send, stat_recv.at[slot], s_send.at[peer], s_recv.at[slot], "ctr", peer)

    @pl.loop(1, n_ctr)
    def _(d):
        s_copy(ctr, ctr_peer(d)).start()

    img[...] = jnp.dot(owned_low, kmat[piece_rows(ctr), :], preferred_element_type=F32)

    @pl.loop(1, half)
    def _(d):
        t = group_at(half - d)
        j = 2 * t + side
        to_group(j, t).wait_recv()
        to_mate(j, af_send.at[t]).start()
        img[...] += jnp.dot(wall[j], kmat[piece_rows(j), :], preferred_element_type=F32)

    to_mate(mate, m_send.at[0]).wait_recv()
    img[...] += jnp.dot(wall[mate], kmat[piece_rows(mate), :], preferred_element_type=F32)

    @pl.loop(1, half)
    def _(d):
        t = group_at(half - d)
        to_mate(2 * t + 1 - side, af_send.at[t]).wait_recv()

    def quarter_cols(p):
        return pl.ds(pl.multiple_of(p * quarter, quarter), quarter)

    def i_copy(p, slot):
        return copy(
            img.at[:, quarter_cols(p)], irecv.at[slot], i_send.at[p], i_recv.at[slot], "pts", p
        )

    def rest(p):
        cols = quarter_cols(p)

        @pl.loop(1, half)
        def _(d):
            j = 2 * group_at(half - d) + 1 - side
            img[:, cols] += jnp.dot(wall[j], kmat[piece_rows(j), cols], preferred_element_type=F32)

    @pl.loop(1, n_pts)
    def _(d):
        p = pts_peer(d)
        rest(p)
        i_copy(p, pts).start()

    rest(pts)
    irecv[pts] = img[:, quarter_cols(pts)]

    @pl.loop(1, n_ctr)
    def _(d):
        j = ctr_peer(n_ctr - d)
        s_copy(j, j).wait_recv()

    stat_sum = lax.fori_loop(1, n_ctr, lambda s, total: total + stat_recv[s], stat_recv[0])
    stat2_send[...] = stat_sum
    stat2_recv[pts] = stat_sum

    def t_copy(slot, peer):
        return copy(stat2_send, stat2_recv.at[slot], t_send.at[peer], t_recv.at[slot], "pts", peer)

    @pl.loop(1, n_pts)
    def _(d):
        t_copy(pts, pts_peer(d)).start()

    @pl.loop(1, n_pts)
    def _(d):
        j = pts_peer(d)
        i_copy(j, j).wait_recv()

    terms = irecv[0]
    for s in range(1, n_pts):
        terms = terms + irecv[s]
    oi[pts] = terms * image_scale + RIDGE_TERM * zvec[:, quarter_cols(pts)]

    def o_copy(slot, peer):
        return copy(oi.at[slot], oi.at[slot], o_send.at[peer], o_recv.at[slot], "pts", peer)

    @pl.loop(1, n_pts)
    def _(d):
        o_copy(pts, pts_peer(d)).start()

    for c in range(m_dev // tile_r):
        cols = slice(c * tile_r, (c + 1) * tile_r)
        prow_out[cols, :] = lax.dot_general(
            k_panel[cols, :], pinv[...], NT, preferred_element_type=F32
        ).astype(BF16)

    @pl.loop(1, n_pts)
    def _(d):
        j = pts_peer(d)
        t_copy(j, j).wait_recv()

    w_total = stat2_recv[0][0:1, :]
    for s in range(1, n_pts):
        w_total = w_total + stat2_recv[s][0:1, :]
    curvature = image_scale / w_scale * w_total + RIDGE_TERM * stat_sum[1:2, :]
    length = stat_sum[2:3, :] / curvature
    length = jnp.broadcast_to(length, (128, 128)).T[:outputs, 0:1]

    @pl.loop(1, n_pts)
    def _(d):
        j = pts_peer(d)
        o_copy(j, j).wait_recv()

    for s in range(n_pts):
        cols = slice(s * quarter, (s + 1) * quarter)
        image_out[:, cols] = oi[s]
        resid_out[:, cols] = residual[:, cols] - length * oi[s]

    @pl.when(ctr == 0)
    def _():
        @pl.loop(1, n_ctr)
        def _(d):
            vals_copy(d).wait_send()
            rows_copy(d).wait_send()

    @pl.loop(1, half)
    def _(d):
        t = group_at(d)
        y_copy(t).wait_send()
        z_copy(t, group).wait_send()
        to_group(ctr, t).wait_send()
        to_mate(2 * t + side, af_send.at[t]).wait_send()

    y_copy(group).wait_send()
    to_mate(ctr, m_send.at[0]).wait_send()

    @pl.loop(1, n_ctr)
    def _(d):
        s_copy(ctr, ctr_peer(d)).wait_send()

    @pl.loop(1, n_pts)
    def _(d):
        p = pts_peer(d)
        vals_pass(pts, p).wait_send()
        rows_pass(pts, p).wait_send()
        pin_copy(pts, p).wait_send()
        i_copy(p, pts).wait_send()
        t_copy(pts, p).wait_send()
        o_copy(pts, p).wait_send()


def relay(*refs):
    count = len(refs) // 2
    for i in range(count):
        refs[count + i][...] = refs[i][...]


def shards(n_ctr, n_pts, points, centers, panel_inverse, direction, residual):
    m_dev, features = centers.shape
    npg = points.shape[0]
    share, panel = panel_inverse.shape
    outputs = direction.shape[0]
    pieces = npg // n_ctr
    quarter = m_dev // n_pts
    half = n_ctr // 2
    vmem = pl.BlockSpec(memory_space=pltpu.VMEM)
    dma = pltpu.SemaphoreType.DMA
    ctr_sem, pts_sem, half_sem = dma((n_ctr,)), dma((n_pts,)), dma((half,))
    piece_set = pltpu.VMEM((half, outputs, pieces), F32)
    sent_set = pltpu.VMEM((half, outputs, pieces), BF16)
    out_shape = (
        jax.ShapeDtypeStruct((m_dev, share), BF16),
        jax.ShapeDtypeStruct((outputs, m_dev), F32),
        jax.ShapeDtypeStruct((outputs, m_dev), F32),
    )
    results = pl.pallas_call(
        functools.partial(step, n_ctr, n_pts),
        out_shape=out_shape,
        in_specs=[vmem] * 5,
        out_specs=(vmem,) * 3,
        scratch_shapes=[
            pltpu.VMEM((npg, m_dev), BF16),
            pltpu.VMEM((2 * features, m_dev), BF16),
            pltpu.VMEM((n_pts, share, features), BF16),
            pltpu.VMEM((n_pts, outputs, share), BF16),
            pltpu.VMEM((n_pts, share, panel), BF16),
            pltpu.VMEM((m_dev, panel), BF16),
            pltpu.VMEM((outputs, m_dev), F32),
            pltpu.VMEM((outputs, m_dev), BF16),
            sent_set, sent_set, piece_set, sent_set, sent_set,
            pltpu.VMEM((n_ctr, outputs, pieces), BF16),
            pltpu.VMEM((8, 128), F32),
            pltpu.VMEM((n_ctr, 8, 128), F32),
            pltpu.VMEM((outputs, m_dev), F32),
            pltpu.VMEM((n_pts, outputs, quarter), F32),
            pltpu.VMEM((n_pts, outputs, quarter), F32),
            pltpu.VMEM((8, 128), F32),
            pltpu.VMEM((n_pts, 8, 128), F32),
            dma((2, n_ctr)), dma((2,)), dma((2, n_pts)), dma((2, n_pts)), pts_sem, pts_sem,
            half_sem, half_sem, half_sem, half_sem, dma((1,)), half_sem, half_sem, ctr_sem,
            ctr_sem, ctr_sem, pts_sem, pts_sem, pts_sem, pts_sem, pts_sem, pts_sem,
        ],
        compiler_params=pltpu.CompilerParams(
            collective_id=0, has_side_effects=True, vmem_limit_bytes=56 * 1024 * 1024
        ),
        cost_estimate=pl.CostEstimate(
            flops=2 * npg * m_dev * (2 * features + 2 * outputs),
            bytes_accessed=4 * npg * features,
            transcendentals=npg * m_dev,
        ),
    )(points, centers, panel_inverse, direction, residual)
    return pl.pallas_call(
        relay,
        out_shape=out_shape,
        in_specs=[vmem] * 3,
        out_specs=(vmem,) * 3,
    )(*results)


def solution(mesh):
    n_ctr, n_pts = mesh.shape["ctr"], mesh.shape["pts"]
    in_specs = (P("pts", None), P("ctr", None), P("pts", None), P(None, "ctr"), P(None, "ctr"))
    out_specs = (P("ctr", "pts"), P(None, "ctr"), P(None, "ctr"))
    return jax.shard_map(
        functools.partial(shards, n_ctr, n_pts),
        mesh=mesh, in_specs=in_specs, out_specs=out_specs, check_vma=False,
    )
```
